256 devices in a mesh: section: 16 (over x_hi, z), dp: 16 (over x_lo, y, core).
Axes of the slice: x: 4 (x_hi: 2, x_lo: 2; x = x_hi * 2 + x_lo), y: 4, z: 8, core: 2. Of those that a mesh axis runs over, the one named last changes fastest.
Arguments:
- stash: bfloat16 [16, 2048, 8192], P('section', 'dp'), may hold values from -6 to 6
- query: bfloat16 [16, 2048, 4096], P('section', 'dp')
- grad_out: bfloat16 [16, 2048, 4096], P('section', 'dp'), may hold values from -6 to 6
- kv_weight: bfloat16 [16, 8192, 1024], P('section', 'dp'), may hold values from -0.0625 to 0.0625
- doc_ids: int32 [16, 2048], P('section', 'dp'), may hold values from 0 to 63, never falling along the last dimension, each value on 1 to 128 neighbouring positions
- evicted: int32 [16], replicated, may hold values from 0 to 1, as said below
Outputs:
- next_grad: bfloat16 [16, 2048, 8192], P('section', 'dp')
- weight_grad: bfloat16 [16, 8192, 1024], P('section', 'dp')
- query_grad: bfloat16 [16, 2048, 4096], P('section', 'dp')
The draws below stay inside these ranges and needn't reach their ends.
Inputs may be any that keep to these rules, and one draw needn't show every extreme that they name: evicted[i] equals evicted[15 - i]; both values occur in every draw. `doc_ids`: never falls along a row.
All inputs are finite; a program needn't handle non-finite values.
Results may differ from the reference program's by a relative error of at most 0.025.
The reference program's roundings to bfloat16 on the way (of `layer_input`, `keyvalue`, `probs`, `grad_scores`, `grad_kv` and `input_grad`) count: a program that leaves them out, or rounds other values in their place, can miss the bound.
Values may be sent and summed in bfloat16 or wider, within the bound.
A program may use at most 128 MiB of HBM per device.

```python
import math
import jax
import jax.numpy as jnp
import numpy as np
from jax import lax

D = 8192
QHEADS = 32
KVHEADS = 4
HEAD_DIM = 128
TOK = 128
TOKENS = 2048
N_SECTION = 16
N_DP = 16


def draw_query(key, part):
    key = jax.random.fold_in(key, 5)
    first_key = jax.random.fold_in(key, 0)
    shape = (N_SECTION, TOKENS, QHEADS * HEAD_DIM)
    values = jax.random.normal(first_key, shape, jnp.float32)
    return values.astype(jnp.bfloat16)


def draw_evicted(key, part):
    key = jax.random.fold_in(key, 11)
    count_key, order_key = jax.random.split(key)
    half_count = N_SECTION // 2
    chosen = jax.random.randint(count_key, (), 1, half_count)
    order = jax.random.permutation(order_key, half_count)
    flags = jnp.where(order < chosen, 1, 0).astype(jnp.int32)
    return jnp.concatenate([flags, flags[::-1]]).astype(jnp.int32)


def shard_levels(key, extent, shards, low, high):
    def one(axis_at, parts):
        steps = jax.random.uniform(jax.random.fold_in(jax.random.fold_in(key, 6), axis_at), (parts,), jnp.float32, low / len(shards), high / len(shards))
        return jnp.repeat(jnp.exp(steps), extent[axis_at] // parts).reshape((-1,) + (1,) * (len(extent) - axis_at - 1))

    gain = one(*shards[0])
    for cut in shards[1:]:
        gain = gain * one(*cut)
    return gain


def length_profile(count, total, reach, skew):
    weights = [(1 << 20) // math.isqrt(standing ** skew) + 1 for standing in range(2, count + 1)]
    surplus, counts = total - reach - (count - 1), [1] * (count - 1)
    while surplus > 0:
        movable = [i for i in range(count - 1) if counts[i] < reach]
        whole, budget = sum([weights[i] for i in movable]), surplus
        for i in movable:
            addition = min(reach - counts[i], max(1, budget * weights[i] // whole), surplus)
            counts[i] = counts[i] + addition
            surplus = surplus - addition
    return np.array([reach] + counts)


def uneven_parts(own_key, amount, total, most, lean):
    if amount == 2:
        one = jax.random.randint(own_key, (), max(1, total - most), min(most, total - 1) + 1)
        return jnp.stack([one, total - one])
    lengths = jnp.asarray(length_profile(amount, total, most, lean), jnp.int32)
    couples = (amount - 1) // 2
    source_of, receiver = lengths[1:1 + 2 * couples:2], lengths[2:2 + 2 * couples:2]
    room = jnp.minimum(source_of - 1, most - receiver)
    moved = jax.random.randint(jax.random.fold_in(own_key, 1), (couples,), 0, 1 << 20) % (room + 1)
    lengths = lengths.at[1:1 + 2 * couples:2].set(source_of - moved).at[2:2 + 2 * couples:2].set(receiver + moved)
    return lengths[jax.random.permutation(jax.random.fold_in(own_key, 2), amount)]


def bell_draw(stream_key, extent, deviation, reach, cuts=(), dtype=jnp.bfloat16):
    array = jax.random.normal(stream_key, extent, jnp.float32) * deviation
    if len(cuts) > 0:
        array = shard_levels(stream_key, extent, cuts, -0.22, 0.18) * array
    return jnp.clip(array, min=-reach, max=reach).astype(dtype)


def setup_inputs(seed: int = 0) -> dict:
    key_of = jax.random.split(jax.random.key(seed), 7)
    stash = bell_draw(key_of[0], (N_SECTION, TOKENS, D), 1.0, 6.0, ((0, 16), (1, 16)))
    query = draw_query(jax.random.fold_in(key_of[6], 71), 0)
    grad_out = bell_draw(key_of[2], (N_SECTION, TOKENS, QHEADS * HEAD_DIM), 1.0, 6.0, ((0, 16), (1, 16)))
    kv_weight = bell_draw(key_of[3], (N_SECTION, D, 2 * KVHEADS * HEAD_DIM), D ** -0.5, 0.0625, ((0, 16), (1, 16)))
    doc_ids = jax.vmap(lambda own: jnp.searchsorted(jnp.cumsum(uneven_parts(own, N_DP * 4, TOKENS, TOK, 1)), jnp.arange(TOKENS), side="right"))(jax.random.split(key_of[4], N_SECTION)).reshape((N_SECTION, TOKENS)).astype(jnp.int32)
    evicted = draw_evicted(jax.random.fold_in(key_of[6], 71), 0)
    return dict(stash=stash, query=query, grad_out=grad_out, kv_weight=kv_weight, doc_ids=doc_ids, evicted=evicted)


def attend_back(queries, upstream, keyvalue, seg_ids):
    tok_count = queries.shape[0]
    group = QHEADS // KVHEADS
    width = KVHEADS * HEAD_DIM
    scale = HEAD_DIM ** -0.5
    q_heads = queries.reshape(tok_count, KVHEADS, group, HEAD_DIM).astype(jnp.float32)
    d_heads = upstream.reshape(tok_count, KVHEADS, group, HEAD_DIM).astype(jnp.float32)
    keys = keyvalue[:, :width].reshape(tok_count, KVHEADS, HEAD_DIM).astype(jnp.float32)
    values = keyvalue[:, width:].reshape(tok_count, KVHEADS, HEAD_DIM).astype(jnp.float32)
    scores = jnp.einsum('ihgd,jhd->hgij', q_heads, keys) * scale
    rows_pos = jnp.arange(tok_count)[:, None]
    cols_pos = jnp.arange(tok_count)[None, :]
    allowed = (seg_ids[:, None] == seg_ids[None, :]) & (cols_pos <= rows_pos)
    scores = jnp.where(allowed, scores, -1e30)
    peak = jnp.max(scores, axis=-1, keepdims=True)
    raised = jnp.exp(scores - peak)
    probs = raised / jnp.sum(raised, axis=-1, keepdims=True)
    probs_low = probs.astype(jnp.bfloat16).astype(jnp.float32)
    output = jnp.einsum('hgij,jhd->ihgd', probs_low, values)
    delta = jnp.einsum('ihgd,ihgd->hgi', d_heads, output)
    grad_values = jnp.einsum('hgij,ihgd->jhd', probs_low, d_heads)
    grad_probs = jnp.einsum('ihgd,jhd->hgij', d_heads, values)
    grad_scores = (probs * (grad_probs - delta[..., None])).astype(jnp.bfloat16).astype(jnp.float32)
    grad_keys = jnp.einsum('hgij,ihgd->jhd', grad_scores, q_heads) * scale
    grad_query = jnp.einsum('hgij,jhd->ihgd', grad_scores, keys) * scale
    grad_kv = jnp.concatenate([grad_keys.reshape(tok_count, width), grad_values.reshape(tok_count, width)], axis=1)
    return grad_kv.astype(jnp.bfloat16), grad_query.reshape(tok_count, QHEADS * HEAD_DIM).astype(jnp.bfloat16)


def one_section(operands):
    layer_input, queries, upstream, weights, seg_ids = operands
    keyvalue = jnp.dot(layer_input, weights, preferred_element_type=jnp.float32).astype(jnp.bfloat16)
    grad_kv, grad_query = jax.vmap(attend_back)(
        queries.reshape(N_DP, TOK, QHEADS * HEAD_DIM),
        upstream.reshape(N_DP, TOK, QHEADS * HEAD_DIM),
        keyvalue.reshape(N_DP, TOK, 2 * KVHEADS * HEAD_DIM),
        seg_ids.reshape(N_DP, TOK))
    grad_kv = grad_kv.reshape(N_DP * TOK, 2 * KVHEADS * HEAD_DIM)
    input_grad = jnp.dot(grad_kv, weights.T, preferred_element_type=jnp.float32).astype(jnp.bfloat16)
    summed = jnp.dot(layer_input.T, grad_kv, preferred_element_type=jnp.float32)
    weight_grad = (summed / N_DP).astype(jnp.bfloat16)
    return input_grad, weight_grad, grad_query.reshape(N_DP * TOK, QHEADS * HEAD_DIM)


def reference(stash, query, grad_out, kv_weight, doc_ids, evicted):
    mirrored = stash[::-1]
    layer_input = jnp.where((evicted == 1)[:, None, None], mirrored, stash)
    input_grads, weight_grads, query_grads = lax.map(one_section, (layer_input, query, grad_out, kv_weight, doc_ids))
    next_grad = jnp.concatenate([input_grads[1:], jnp.zeros_like(input_grads[:1])], axis=0)
    return next_grad, weight_grads, query_grads
```

```python
import jax
import jax.numpy as jnp
from jax import lax
from jax.sharding import PartitionSpec as P

QHEADS = 32
KVHEADS = 4
HEAD_DIM = 128


def mirrored(block, axis):
    count = lax.axis_size(axis)
    return lax.ppermute(block, axis, [(i, count - 1 - i) for i in range(count)])


def shifted(array, axis, by):
    count = lax.axis_size(axis)
    pairs = [(i, i + by) for i in range(count) if 0 <= i + by < count]
    return lax.ppermute(array, axis, pairs)


def attend_back(queries, upstream, keyvalue, seg_ids):
    tok_count = queries.shape[0]
    group = QHEADS // KVHEADS
    width = KVHEADS * HEAD_DIM
    scale = HEAD_DIM ** (-0.5)
    q_heads = queries.reshape(tok_count, KVHEADS, group, HEAD_DIM)
    d_heads = upstream.reshape(tok_count, KVHEADS, group, HEAD_DIM)
    keys = keyvalue[:, :width].reshape(tok_count, KVHEADS, HEAD_DIM)
    values = keyvalue[:, width:].reshape(tok_count, KVHEADS, HEAD_DIM)
    scores = jnp.einsum("ihgd,jhd->hgij", q_heads, keys, preferred_element_type=jnp.float32) * scale
    rows_pos = jnp.arange(tok_count)[:, None]
    cols_pos = jnp.arange(tok_count)[None, :]
    allowed = (seg_ids[:, None] == seg_ids[None, :]) & (cols_pos <= rows_pos)
    scores = jnp.where(allowed, scores, -1e30)
    peak = jnp.max(scores, axis=-1, keepdims=True)
    raised = jnp.exp(scores - peak)
    probs = raised / jnp.sum(raised, axis=-1, keepdims=True)
    probs_low = probs.astype(jnp.bfloat16)
    output = jnp.einsum("hgij,jhd->ihgd", probs_low, values, preferred_element_type=jnp.float32)
    delta = jnp.einsum("ihgd,ihgd->hgi", d_heads.astype(jnp.float32), output)
    grad_values = jnp.einsum(
        "hgij,ihgd->jhd", probs_low, d_heads, preferred_element_type=jnp.float32
    )
    grad_probs = jnp.einsum("ihgd,jhd->hgij", d_heads, values, preferred_element_type=jnp.float32)
    grad_scores = (probs * (grad_probs - delta[..., None])).astype(jnp.bfloat16)
    grad_keys = (
        jnp.einsum("hgij,ihgd->jhd", grad_scores, q_heads, preferred_element_type=jnp.float32)
        * scale
    )
    grad_query = (
        jnp.einsum("hgij,jhd->ihgd", grad_scores, keys, preferred_element_type=jnp.float32) * scale
    )
    grad_kv = jnp.concatenate(
        [grad_keys.reshape(tok_count, width), grad_values.reshape(tok_count, width)], axis=1
    )
    return (
        grad_kv.astype(jnp.bfloat16),
        grad_query.reshape(tok_count, QHEADS * HEAD_DIM).astype(jnp.bfloat16),
    )


def local(stash, query, grad_out, kv_weight, doc_ids, evicted):
    held_slot = stash[0]
    queries = query[0]
    upstream = grad_out[0]
    weight_shard = kv_weight[0]
    seg_ids = doc_ids[0]
    fetched = mirrored(held_slot, "section")
    position = lax.axis_index("section")
    layer_input = jnp.where(evicted[position] == 1, fetched, held_slot)
    replicas = lax.axis_size("dp")
    x_columns = lax.all_to_all(layer_input, "dp", split_axis=1, concat_axis=0, tiled=True)
    x_part = x_columns
    keyvalue = lax.psum_scatter(
        jnp.dot(x_part, weight_shard, preferred_element_type=jnp.float32),
        "dp",
        scatter_dimension=0,
        tiled=True,
    ).astype(jnp.bfloat16)
    grad_kv, grad_query = attend_back(queries, upstream, keyvalue, seg_ids)
    portion = lax.all_gather(grad_kv, "dp", axis=0, tiled=True)
    x_part = x_columns
    grad_sum = jnp.einsum("tc,tk->ck", x_part, portion, preferred_element_type=jnp.float32)
    rows_grad = jnp.einsum("tk,ck->tc", portion, weight_shard, preferred_element_type=jnp.float32)
    input_cols = rows_grad.astype(jnp.bfloat16)
    weight_total, input_cols = (grad_sum, input_cols)
    input_grad = lax.all_to_all(input_cols, "dp", split_axis=0, concat_axis=1, tiled=True)
    weight_out = (weight_total / replicas).astype(jnp.bfloat16)
    passed = shifted(input_grad, "section", -1)
    return (passed[None], weight_out[None], grad_query[None])


def solution(mesh):
    placed = (
        P("section", "dp", None),
        P("section", "dp", None),
        P("section", "dp", None),
        P("section", "dp", None),
        P("section", "dp"),
        P(),
    )
    return jax.shard_map(
        local,
        mesh=mesh,
        in_specs=placed,
        out_specs=(P("section", "dp", None), P("section", "dp", None), P("section", "dp", None)),
        check_vma=False,
    )
```

```python
import jax
import jax.numpy as jnp
from jax import lax
from jax.experimental import pallas as pl
from jax.experimental.pallas import tpu as pltpu
from jax.sharding import PartitionSpec as P

QHEADS = 32
KVHEADS = 4
HEAD_DIM = 128
GROUP = QHEADS // KVHEADS
WIDTH = KVHEADS * HEAD_DIM
MESH = pl.DeviceIdType.MESH
MIB = 1024 * 1024
N_DP = 16
N_SENDS = 30


def remote(src, dst, send_sem, recv_sem, target):
    return pltpu.make_async_remote_copy(
        src_ref=src,
        dst_ref=dst,
        send_sem=send_sem,
        recv_sem=recv_sem,
        device_id=target,
        device_id_type=MESH,
    )


class Gather:
    def __init__(self, own_half, buf, send_sem, recv_sem):
        self.own_half, self.buf = own_half, buf
        self.send_sem, self.recv_sem = send_sem, recv_sem
        self.sent = []
        me = lax.axis_index("dp")
        x, y, core = me // 8, (me % 8) // 2, me % 2
        at = lambda far, step, other: (
            (1 - x if far else x) * 8
            + lax.rem(y + step, 4) * 2
            + (1 - core if other else core)
        )
        self.at = at
        self.me = me
        self.up, self.down = at(0, 1, 0), at(0, 3, 0)
        self.across, self.sibling = at(1, 0, 0), at(0, 0, 1)

    def slot(self, far, step, half, other=0):
        return self.at(far, step, other) * 2 + half

    def send(self, slot, target, src=None):
        where = self.buf.at[slot]
        copy = remote(
            where if src is None else src,
            where,
            self.send_sem.at[len(self.sent)],
            self.recv_sem.at[slot],
            {"dp": target},
        )
        copy.start()
        self.sent.append(copy)

    def wait(self, slot):
        where = self.buf.at[slot]
        remote(where, where, self.send_sem.at[0], self.recv_sem.at[slot], {"dp": self.up}).wait_recv()

    def start(self):
        for half in range(2):
            slot, src = self.slot(0, 0, half), self.own_half(half)
            for target in (self.across, self.up, self.down, self.sibling):
                self.send(slot, target, src)

    def forward(self, far, step, half, targets):
        slot = self.slot(far, step, half)
        self.wait(slot)
        for target in targets:
            self.send(slot, target)

    def relay(self):
        up, down, sibling = self.up, self.down, self.sibling
        self.forward(0, 3, 0, (up, sibling))
        self.forward(0, 1, 0, (sibling,))
        self.forward(1, 0, 0, (up, down, sibling))
        self.forward(0, 1, 1, (down, sibling))
        self.forward(0, 3, 1, (sibling,))
        self.forward(1, 0, 1, (up, down, sibling))
        self.forward(0, 2, 0, (sibling,))
        self.forward(0, 2, 1, (sibling,))
        self.forward(1, 3, 0, (up, sibling))
        self.forward(1, 1, 0, (sibling,))
        self.forward(1, 1, 1, (down, sibling))
        self.forward(1, 3, 1, (sibling,))
        self.forward(1, 2, 0, (sibling,))
        self.forward(1, 2, 1, (sibling,))

    def finish(self):
        for far in range(2):
            for step in range(4):
                for half in range(2):
                    self.wait(self.slot(far, step, half, 1))

    def drain(self):
        for copy in self.sent:
            copy.wait_send()


def greet(targets):
    barrier = pltpu.get_barrier_semaphore()
    for target in targets:
        pl.semaphore_signal(barrier, inc=1, device_id=target, device_id_type=MESH)
    pl.semaphore_wait(barrier, len(targets))


def columns(index, width):
    return pl.ds(pl.multiple_of(index * width, width), width)


def pre_kernel(
    stash_ref, weight_ref, evicted_ref, x_ref, whole_ref, kv_ref,
    wbuf, fetched, held, xbuf, total,
    w_send, w_recv, m_send, m_recv, local_sem,
):
    section = lax.axis_index("section")
    mirror = {"section": 15 - section}
    depth = weight_ref.shape[0]
    half_rows = depth // 2
    gather = Gather(lambda half: weight_ref.at[pl.ds(half * half_rows, half_rows)], wbuf, w_send, w_recv)
    me = gather.me
    greet([mirror] + [{"dp": t} for t in (gather.up, gather.down, gather.across, gather.sibling)])
    gather.start()

    def mirrored(chunk):
        at = columns(chunk, depth)
        return remote(stash_ref.at[:, at], fetched.at[:, at], m_send.at[chunk], m_recv.at[chunk], mirror)

    for chunk in range(N_DP):
        mirrored(chunk).start()
    own_copies = [
        pltpu.make_async_copy(weight_ref.at[pl.ds(h * half_rows, half_rows)], wbuf.at[2 * me + h], local_sem.at[h])
        for h in range(2)
    ]
    held_copy = pltpu.make_async_copy(stash_ref, held, local_sem.at[2])
    for copy in own_copies:
        copy.start()
    held_copy.start()
    for copy in own_copies:
        copy.wait()
    held_copy.wait()
    gather.relay()
    gather.finish()
    whole_copy = pltpu.make_async_copy(wbuf, whole_ref, local_sem.at[3])
    whole_copy.start()

    total[...] = jnp.zeros_like(total)
    moved = evicted_ref[section] == 1

    @pl.loop(0, N_DP)
    def _(chunk):
        at = columns(chunk, depth)
        mirrored(chunk).wait_recv()
        part = jnp.where(moved, fetched[:, at], held[:, at])
        xbuf[:, at] = part
        for half in range(2):
            total[...] += jnp.dot(
                part[:, half * half_rows:(half + 1) * half_rows],
                wbuf[2 * chunk + half],
                preferred_element_type=jnp.float32,
            )

    x_copy = pltpu.make_async_copy(xbuf, x_ref, local_sem.at[4])
    x_copy.start()
    kv_ref[...] = total[...].astype(kv_ref.dtype)

    @pl.loop(0, N_DP)
    def _(chunk):
        mirrored(chunk).wait_send()

    gather.drain()
    x_copy.wait()
    whole_copy.wait()


def pre(stash, weight, evicted):
    tok, features = stash.shape
    depth, width = weight.shape
    bf16 = jnp.bfloat16
    any_space = pl.BlockSpec(memory_space=pl.ANY)
    return pl.pallas_call(
        pre_kernel,
        out_shape=(
            jax.ShapeDtypeStruct((tok, features), bf16),
            jax.ShapeDtypeStruct((2 * N_DP, depth // 2, width), bf16),
            jax.ShapeDtypeStruct((tok, width), bf16),
        ),
        in_specs=[any_space, any_space, pl.BlockSpec(memory_space=pltpu.SMEM)],
        out_specs=(any_space, any_space, pl.BlockSpec(memory_space=pltpu.VMEM)),
        scratch_shapes=[
            pltpu.VMEM((2 * N_DP, depth // 2, width), bf16),
            pltpu.VMEM((tok, features), bf16),
            pltpu.VMEM((tok, features), bf16),
            pltpu.VMEM((tok, features), bf16),
            pltpu.VMEM((tok, width), jnp.float32),
            pltpu.SemaphoreType.DMA((N_SENDS,)),
            pltpu.SemaphoreType.DMA((2 * N_DP,)),
            pltpu.SemaphoreType.DMA((N_DP,)),
            pltpu.SemaphoreType.DMA((N_DP,)),
            pltpu.SemaphoreType.DMA((5,)),
        ],
        compiler_params=pltpu.CompilerParams(
            collective_id=0, has_side_effects=True, vmem_limit_bytes=48 * MIB
        ),
        name="pre",
    )(stash, weight, evicted)


def attend_kernel(q_ref, d_ref, kv_ref, col_ref, row_ref, dq_ref, g_ref):
    head = pl.program_id(0)
    tok = q_ref.shape[0]
    scale = HEAD_DIM ** -0.5
    at_k = columns(head, HEAD_DIM)
    at_v = pl.ds(pl.multiple_of(WIDTH + head * HEAD_DIM, HEAD_DIM), HEAD_DIM)
    keys, values = kv_ref[:, at_k], kv_ref[:, at_v]
    stack = lambda ref: jnp.concatenate(
        [ref[:, h * HEAD_DIM:(h + 1) * HEAD_DIM] for h in range(GROUP)], axis=0
    )
    f32 = jnp.float32
    nt = lambda a, b: lax.dot_general(a, b, (((1,), (1,)), ((), ())), preferred_element_type=f32)
    tn = lambda a, b: lax.dot_general(a, b, (((0,), (0,)), ((), ())), preferred_element_type=f32)
    queries, upstream = stack(q_ref), stack(d_ref)
    rows = lax.broadcasted_iota(jnp.int32, (tok, tok), 0)
    cols = lax.broadcasted_iota(jnp.int32, (tok, tok), 1)
    allowed = (col_ref[...] == row_ref[...]) & (cols <= rows)
    scores = (nt(queries, keys) * scale).reshape(GROUP, tok, tok)
    scores = jnp.where(allowed[None], scores, -1e30).reshape(GROUP * tok, tok)
    raised = jnp.exp(scores - jnp.max(scores, axis=-1, keepdims=True))
    probs = raised / jnp.sum(raised, axis=-1, keepdims=True)
    probs_low = probs.astype(jnp.bfloat16)
    output = jnp.dot(probs_low, values, preferred_element_type=f32)
    delta = jnp.sum(upstream.astype(f32) * output, axis=-1, keepdims=True)
    grad_scores = (probs * (nt(upstream, values) - delta)).astype(jnp.bfloat16)
    g_ref[:, at_k] = (tn(grad_scores, queries) * scale).astype(g_ref.dtype)
    g_ref[:, at_v] = tn(probs_low, upstream).astype(g_ref.dtype)
    dq = jnp.dot(grad_scores, keys, preferred_element_type=f32) * scale
    for h in range(GROUP):
        dq_ref[:, h * HEAD_DIM:(h + 1) * HEAD_DIM] = dq[h * tok:(h + 1) * tok].astype(dq_ref.dtype)


def attend(queries, upstream, keyvalue, seg_ids):
    tok = queries.shape[0]
    wide = pl.BlockSpec((tok, GROUP * HEAD_DIM), lambda h: (0, h))
    whole = lambda *shape: pl.BlockSpec(shape, lambda h: (0, 0))
    return pl.pallas_call(
        attend_kernel,
        grid=(KVHEADS,),
        out_shape=(
            jax.ShapeDtypeStruct(queries.shape, jnp.bfloat16),
            jax.ShapeDtypeStruct(keyvalue.shape, jnp.bfloat16),
        ),
        in_specs=[wide, wide, whole(*keyvalue.shape), whole(tok, 1), whole(1, tok)],
        out_specs=(wide, whole(*keyvalue.shape)),
        compiler_params=pltpu.CompilerParams(
            dimension_semantics=("arbitrary",), vmem_limit_bytes=48 * MIB
        ),
        name="attend",
    )(queries, upstream, keyvalue, seg_ids.reshape(tok, 1), seg_ids.reshape(1, tok))


def post_kernel(
    x_ref, whole_ref, g_ref, passed_ref, wgrad_ref,
    wbuf, gbuf, xcols, rows,
    g_send, g_recv, x_send, x_recv, s_send, s_recv, load_sem, local_sem,
):
    section = lax.axis_index("section")
    tok, width = g_ref.shape
    half_rows = wbuf.shape[1]
    depth = 2 * half_rows
    below = {"section": lax.rem(section + 15, 16)}
    above = {"section": lax.rem(section + 1, 16)}
    half_tok = tok // 2
    gather = Gather(lambda half: g_ref.at[pl.ds(half * half_tok, half_tok)], gbuf, g_send, g_recv)
    me = gather.me
    others = [{"dp": lax.rem(me + k, N_DP)} for k in range(1, N_DP)]

    def load(chunk):
        at = pl.ds(2 * chunk, 2)
        return pltpu.make_async_copy(whole_ref.at[at], wbuf.at[at], load_sem.at[chunk])

    for chunk in range(N_DP):
        load(chunk).start()
    own_copies = [
        pltpu.make_async_copy(g_ref.at[pl.ds(h * half_tok, half_tok)], gbuf.at[2 * me + h], local_sem.at[h])
        for h in range(2)
    ]
    own_x = pltpu.make_async_copy(x_ref.at[:, columns(me, depth)], xcols.at[me], local_sem.at[2])
    for copy in own_copies + [own_x]:
        copy.start()
    greet([below, above] + others)
    gather.start()

    def shifted(chunk):
        at = columns(chunk, depth)
        return remote(rows.at[:, at], passed_ref.at[:, at], s_send.at[chunk], s_recv.at[chunk], below)

    @pl.loop(0, N_DP)
    def _(chunk):
        load(chunk).wait()
        for half in range(2):
            at = pl.ds(pl.multiple_of(chunk * depth + half * half_rows, half_rows), half_rows)
            rows[:, at] = lax.dot_general(
                g_ref[...], wbuf[2 * chunk + half], (((1,), (1,)), ((), ())),
                preferred_element_type=jnp.float32,
            ).astype(rows.dtype)
        shifted(chunk).start()

    exchanged = []
    for k, other in zip(range(1, N_DP), others):
        copy = remote(
            x_ref.at[:, columns(other["dp"], depth)], xcols.at[me], x_send.at[k], x_recv.at[k], other
        )
        copy.start()
        exchanged.append(copy)
    gather.relay()
    gather.finish()
    for copy in own_copies + [own_x]:
        copy.wait()
    for k in range(1, N_DP):
        source = lax.rem(me + N_DP - k, N_DP)
        remote(
            xcols.at[source], xcols.at[source], x_send.at[k], x_recv.at[k], {"dp": source}
        ).wait_recv()

    whole_x = xcols[...].reshape(N_DP * tok, depth)
    whole_g = gbuf[...].reshape(N_DP * tok, width)
    for half in range(2):
        at = slice(half * half_rows, (half + 1) * half_rows)
        summed = lax.dot_general(
            whole_x[:, at], whole_g, (((0,), (0,)), ((), ())), preferred_element_type=jnp.float32
        )
        wgrad_ref[at, :] = (summed * (1.0 / N_DP)).astype(wgrad_ref.dtype)

    for copy in exchanged:
        copy.wait_send()
    gather.drain()

    @pl.loop(0, N_DP)
    def _(chunk):
        shifted(chunk).wait()


def post(x, whole, grad_kv):
    tok, features = x.shape
    blocks, half_rows, width = whole.shape
    bf16 = jnp.bfloat16
    any_space = pl.BlockSpec(memory_space=pl.ANY)
    vmem = pl.BlockSpec(memory_space=pltpu.VMEM)
    dma = pltpu.SemaphoreType.DMA
    return pl.pallas_call(
        post_kernel,
        out_shape=(
            jax.ShapeDtypeStruct((tok, features), bf16),
            jax.ShapeDtypeStruct((2 * half_rows, width), bf16),
        ),
        in_specs=[any_space, any_space, vmem],
        out_specs=(any_space, vmem),
        scratch_shapes=[
            pltpu.VMEM((blocks, half_rows, width), bf16),
            pltpu.VMEM((blocks, tok // 2, width), bf16),
            pltpu.VMEM((N_DP, tok, 2 * half_rows), bf16),
            pltpu.VMEM((tok, features), bf16),
            dma((N_SENDS,)), dma((blocks,)),
            dma((N_DP,)), dma((N_DP,)),
            dma((N_DP,)), dma((N_DP,)),
            dma((N_DP,)), dma((3,)),
        ],
        compiler_params=pltpu.CompilerParams(
            collective_id=1, has_side_effects=True, vmem_limit_bytes=48 * MIB
        ),
        name="post",
    )(x, whole, grad_kv)


def local(stash, query, grad_out, kv_weight, doc_ids, evicted):
    x, whole, keyvalue = pre(stash[0], kv_weight[0], evicted)
    grad_query, grad_kv = attend(query[0], grad_out[0], keyvalue, doc_ids[0])
    passed, weight_out = post(x, whole, grad_kv)
    last = lax.axis_index("section") == lax.axis_size("section") - 1
    passed = jnp.where(last, jnp.zeros_like(passed), passed)
    return (passed[None], weight_out[None], grad_query[None])


def solution(mesh):
    rows = P("section", "dp", None)
    return jax.shard_map(
        local,
        mesh=mesh,
        in_specs=(rows, rows, rows, rows, P("section", "dp"), P()),
        out_specs=(rows, rows, rows),
        check_vma=False,
    )
```
